32 devices in a mesh: frame: 8 (over y, x, core), tensor: 4 (over z).
Axes of the slice: x: 2, y: 2, z: 4, core: 2. Of those that a mesh axis runs over, the one named last changes fastest.
Arguments:
- latents: bfloat16 [4096, 5120], P('frame', 'tensor'), may hold values from -6 to 6
- w_query: bfloat16 [5120, 3072], P(None, 'tensor'), may hold values from -0.078125 to 0.078125
- w_key: bfloat16 [5120, 3072], P(None, 'tensor'), may hold values from -0.078125 to 0.078125
- w_value: bfloat16 [5120, 3072], P(None, 'tensor'), may hold values from -0.078125 to 0.078125
- w_out: bfloat16 [3072, 5120], P('tensor'), may hold values from -0.109375 to 0.109375
- query_gain: float32 [24, 128], P('tensor'), may hold values from 0.5 to 14, as said below
- key_gain: float32 [24, 128], P('tensor'), may hold values from 0.5 to 14, as said below
- mod_table: float32 [16, 3, 5120], replicated, may hold values from -3 to 3
- levels: int32 [8], P('frame'), may hold values from 0 to 15
- span_counts: int32 [8], replicated, may hold values from 1 to 512, 3072 in all
- block_mask: int32 [8, 8], P('frame'), may hold values 0 or 1
- span_order: int32 [8], replicated, may hold values from 0 to 7, each once
Outputs:
- updated: bfloat16 [4096, 5120], P('frame', 'tensor')
The draws below stay inside these ranges and needn't reach their ends.
Inputs may be any that keep to these rules, and one draw needn't show every extreme that they name: `query_gain`: gains are positive. `key_gain`: gains are positive. `span_order`: each rank appears once.
All inputs are finite; a program needn't handle non-finite values. No bound on the sum of `block_mask` on one device may be relied on, other than what follows from the above.
Results may differ from the reference program's by a relative error of at most 0.012.
The reference program's roundings to bfloat16 on the way count: a program that leaves them out, or rounds other values in their place, can miss the bound.
Values may be sent and summed in bfloat16 or wider, within the bound.
A program may use at most 128 MiB of HBM per device.

```python
import math
import jax
import jax.numpy as jnp
import numpy as np
from jax import lax

D = 5120
HEADS = 24
HEAD_DIM = 128
LEVELS = 16
ROWS = 512
SPANS = 8
TOKENS = 4096
N_TENSOR = 4


def gain_values(key, salt):
    own_key = jax.random.fold_in(key, salt)
    gain_table = jnp.exp(jax.random.uniform(own_key, (HEADS, HEAD_DIM), jnp.float32, math.log(0.5), math.log(2.0)))
    return gain_table


def draw_query_gain(key, part):
    return gain_values(key, 11)


def draw_key_gain(key, part):
    return gain_values(key, 23)


def place_ends(values, stream_key, least, largest):
    index_at = [jax.random.randint(jax.random.fold_in(stream_key, axis), (), 0, length) for axis, length in enumerate(values.shape)]
    main_axis = values.shape.index(max(values.shape))
    beside = index_at[:main_axis] + [(index_at[main_axis] + 1) % values.shape[main_axis]] + index_at[main_axis + 1:]
    return values.at[tuple(index_at)].set(least).at[tuple(beside)].set(largest)


def shard_levels(rng, extent, split, smallest, top_value):
    level, own = 1.0, jax.random.fold_in(rng, 6)
    for dim, parts in split:
        steps = jnp.exp(jax.random.uniform(jax.random.fold_in(own, dim), (parts,), jnp.float32, smallest / len(split), top_value / len(split)))
        level = level * jnp.repeat(steps, extent[dim] // parts).reshape([-1 if axis == dim else 1 for axis in range(len(extent))])
    return level


def profile(amount, total, reach, slope):
    portions = [(1 << 20) // math.isqrt(standing ** slope) + 1 for standing in range(2, amount + 1)]
    spare, holding = total - reach - (amount - 1), [1] * (amount - 1)
    while spare > 0:
        movable = [i for i in range(amount - 1) if holding[i] < reach]
        mass, remaining = sum([portions[i] for i in movable]), spare
        for i in movable:
            addition = min(reach - holding[i], max(1, remaining * portions[i] // mass), spare)
            holding[i] = holding[i] + addition
            spare = spare - addition
    return np.array([reach] + holding)


def uneven_parts(rng, number_of, total, reach, skew):
    if number_of == 2:
        one = jax.random.randint(rng, (), max(1, total - reach), min(reach, total - 1) + 1)
        return jnp.stack([one, total - one])
    sizes = jnp.asarray(profile(number_of, total, reach, skew), jnp.int32)
    twos = (number_of - 1) // 2
    giver, taker = sizes[1:1 + 2 * twos:2], sizes[2:2 + 2 * twos:2]
    slack = jnp.minimum(giver - 1, reach - taker)
    moved = jax.random.randint(jax.random.fold_in(rng, 1), (twos,), 0, 1 << 20) % (slack + 1)
    sizes = sizes.at[1:1 + 2 * twos:2].set(giver - moved).at[2:2 + 2 * twos:2].set(taker + moved)
    return sizes[jax.random.permutation(jax.random.fold_in(rng, 2), number_of)]


def noise(key, extent, deviation, most, split=(), kind=jnp.bfloat16):
    entries = jax.random.normal(key, extent, jnp.float32) * deviation
    if len(split) > 0:
        entries = shard_levels(key, extent, split, -0.22, 0.18) * entries
    return jnp.clip(entries, min=-most, max=most).astype(kind)


def setup_inputs(seed: int = 0) -> dict:
    seeds = jax.random.split(jax.random.key(seed), 13)
    latents = noise(seeds[0], (TOKENS, D), 1.0, 6.0, ((0, 8), (1, 4)))
    w_query = noise(seeds[1], (D, HEADS * HEAD_DIM), D ** -0.5, 0.078125, ((1, 4),))
    w_key = noise(seeds[2], (D, HEADS * HEAD_DIM), D ** -0.5, 0.078125, ((1, 4),))
    w_value = noise(seeds[3], (D, HEADS * HEAD_DIM), D ** -0.5, 0.078125, ((1, 4),))
    w_out = noise(seeds[4], (HEADS * HEAD_DIM, D), (HEADS * HEAD_DIM) ** -0.5, 0.109375, ((0, 4),))
    query_gain = draw_query_gain(jax.random.fold_in(seeds[12], 71), 0)
    key_gain = draw_key_gain(jax.random.fold_in(seeds[12], 71), 0)
    mod_table = noise(seeds[7], (LEVELS, 3, D), 0.5, 3.0, (), jnp.float32)
    levels = place_ends(jax.random.randint(seeds[8], (SPANS,), 0, LEVELS), jax.random.fold_in(seeds[8], 1), 0, LEVELS - 1).astype(jnp.int32)
    span_counts = uneven_parts(seeds[9], SPANS, 3 * ROWS * SPANS // 4, ROWS, 1).astype(jnp.int32)
    block_mask = place_ends((jax.random.randint(seeds[10], (SPANS, SPANS), 0, 4) < 3).astype(jnp.int32), jax.random.fold_in(seeds[10], 1), 0, 1)
    span_order = jax.random.permutation(seeds[11], SPANS).astype(jnp.int32)
    return dict(latents=latents, w_query=w_query, w_key=w_key, w_value=w_value, w_out=w_out, query_gain=query_gain, key_gain=key_gain, mod_table=mod_table, levels=levels, span_counts=span_counts, block_mask=block_mask, span_order=span_order)


EPSILON = 1e-06
NEG_FILL = -1e+30

def head_norm(projection, gain_table):
    shaped = projection.reshape(TOKENS, HEADS, HEAD_DIM)
    scaled = shaped * lax.rsqrt(lax.optimization_barrier(jnp.mean(shaped * shaped, axis=-1, keepdims=True)) + EPSILON) * gain_table
    return scaled.astype(jnp.bfloat16)

def reference(latents, w_query, w_key, w_value, w_out, query_gain, key_gain, mod_table, levels, span_counts, block_mask, span_order):
    modulation = mod_table[levels]
    shift = jnp.repeat(modulation[:, 0], ROWS, axis=0)
    scale = jnp.repeat(modulation[:, 1], ROWS, axis=0)
    gate = jnp.repeat(modulation[:, 2], ROWS, axis=0)
    floats = latents.astype(jnp.float32)
    row_mean = lax.optimization_barrier(jnp.mean(floats, axis=1, keepdims=True))
    row_square = lax.optimization_barrier(jnp.mean(floats * floats, axis=1, keepdims=True))
    normed = ((floats - row_mean) * lax.rsqrt(row_square - row_mean * row_mean + EPSILON) * (1.0 + scale) + shift).astype(jnp.bfloat16)
    queries = head_norm(jnp.dot(normed, w_query, preferred_element_type=jnp.float32), query_gain)
    keys_all = head_norm(jnp.dot(normed, w_key, preferred_element_type=jnp.float32), key_gain)
    values_all = jnp.dot(normed, w_value, preferred_element_type=jnp.float32).astype(jnp.bfloat16).reshape(TOKENS, HEADS, HEAD_DIM)
    span_ids = jnp.arange(SPANS, dtype=jnp.int32)
    ranks = span_order
    slot_ids = jnp.arange(TOKENS, dtype=jnp.int32)
    key_span = slot_ids // ROWS
    key_live = slot_ids % ROWS < span_counts[key_span]
    keys_float = keys_all.astype(jnp.float32)
    values_float = values_all.astype(jnp.float32)
    score_factor = 1.0 / HEAD_DIM ** 0.5

    def one_span(span):
        start = (span * ROWS).astype(jnp.int32)
        query_block = lax.dynamic_slice_in_dim(queries, start, ROWS, 0).astype(jnp.float32)
        linked = (block_mask[span][key_span] == 1) | (key_span == span)
        allowed = (ranks[key_span] <= ranks[span]) & linked & key_live
        scores = jnp.einsum('qhd,khd->hqk', query_block, keys_float) * score_factor
        scores = jnp.where(allowed[None, None, :], scores, NEG_FILL)
        top = lax.optimization_barrier(jnp.max(scores, axis=-1, keepdims=True))
        weights = jnp.where(allowed[None, None, :], jnp.exp(scores - top), 0.0)
        total = lax.optimization_barrier(jnp.sum(weights, axis=-1))
        rounded = weights.astype(jnp.bfloat16).astype(jnp.float32)
        summed = jnp.einsum('hqk,khd->qhd', rounded, values_float)
        attended = summed / jnp.transpose(total)[:, :, None]
        return attended.astype(jnp.bfloat16).reshape(ROWS, HEADS * HEAD_DIM)
    attended = lax.map(one_span, span_ids).reshape(TOKENS, HEADS * HEAD_DIM)
    group_width = HEADS * HEAD_DIM // N_TENSOR
    projected = jnp.zeros((TOKENS, D), jnp.float32)
    for group in range(N_TENSOR):
        term = jnp.dot(attended[:, group * group_width:(group + 1) * group_width], w_out[group * group_width:(group + 1) * group_width], preferred_element_type=jnp.float32)
        term = lax.optimization_barrier(term.astype(jnp.bfloat16))
        projected = projected + term.astype(jnp.float32)
    return (floats + gate * projected).astype(jnp.bfloat16)
```

```python
import functools
import math

import jax
import jax.numpy as jnp
from jax import lax
from jax.experimental import pallas as pl
from jax.experimental.pallas import tpu as pltpu
from jax.sharding import PartitionSpec as P

HEAD_DIM = 128
EPSILON = 1e-06
NEG_FILL = -1e30
GATHER_PARTS = 4
QUERY_PARTS = 2
VMEM_BYTES = 56 * 1024 * 1024
FACTOR = math.log2(math.e) / math.sqrt(HEAD_DIM)


def qkv_kernel(x_ref, shift_ref, scale_ref, wq_ref, wk_ref, wv_ref, qg_ref, kg_ref, q_ref, kv_ref, normed_ref):
    shards, rows, width = x_ref.shape
    heads = q_ref.shape[0]

    @pl.when(pl.program_id(0) == 0)
    def _():
        total = jnp.zeros((rows, 1), jnp.float32)
        square = jnp.zeros((rows, 1), jnp.float32)
        for t in range(shards):
            x = x_ref[t].astype(jnp.float32)
            total += jnp.sum(x, axis=1, keepdims=True)
            square += jnp.sum(x * x, axis=1, keepdims=True)
        mean = total / (shards * width)
        inverse = lax.rsqrt(square / (shards * width) - mean * mean + EPSILON)
        for t in range(shards):
            columns = slice(t * width, (t + 1) * width)
            x = x_ref[t].astype(jnp.float32)
            y = (x - mean) * inverse * (1.0 + scale_ref[:, columns]) + shift_ref[:, columns]
            normed_ref[:, columns] = y.astype(jnp.bfloat16)

    normed = normed_ref[...]

    def head_norm(shaped, gain):
        power = jnp.mean(shaped * shaped, axis=-1, keepdims=True)
        return (shaped * lax.rsqrt(power + EPSILON) * gain).astype(jnp.bfloat16)

    q = jnp.dot(normed, wq_ref[...], preferred_element_type=jnp.float32)
    k = jnp.dot(normed, wk_ref[...], preferred_element_type=jnp.float32)
    v = jnp.dot(normed, wv_ref[...], preferred_element_type=jnp.float32).astype(jnp.bfloat16)
    for h in range(heads):
        columns = slice(h * HEAD_DIM, (h + 1) * HEAD_DIM)
        q_ref[h] = head_norm(q[:, columns], qg_ref[h])
        kv_ref[0, h] = head_norm(k[:, columns], kg_ref[h])
        kv_ref[1, h] = v[:, columns]


def qkv(x, shift, scale, wq, wk, wv, qg, kg):
    shards, rows, width = x.shape
    model = shards * width
    heads = wq.shape[1] // HEAD_DIM
    step = 2 if heads % 2 == 0 else 1
    weight = pl.BlockSpec((model, step * HEAD_DIM), lambda h: (0, h))
    gain = pl.BlockSpec((step, 1, HEAD_DIM), lambda h: (h, 0, 0))
    row = pl.BlockSpec((1, model), lambda h: (0, 0))
    return pl.pallas_call(
        qkv_kernel,
        grid=(heads // step,),
        in_specs=[pl.BlockSpec((shards, rows, width), lambda h: (0, 0, 0)), row, row, weight, weight, weight, gain, gain],
        out_specs=[
            pl.BlockSpec((step, rows, HEAD_DIM), lambda h: (h, 0, 0)),
            pl.BlockSpec((2, step, rows, HEAD_DIM), lambda h: (0, h, 0, 0)),
        ],
        out_shape=[
            jax.ShapeDtypeStruct((heads, rows, HEAD_DIM), jnp.bfloat16),
            jax.ShapeDtypeStruct((2, heads, rows, HEAD_DIM), jnp.bfloat16),
        ],
        scratch_shapes=[pltpu.VMEM((rows, model), jnp.bfloat16)],
        compiler_params=pltpu.CompilerParams(vmem_limit_bytes=VMEM_BYTES),
        cost_estimate=pl.CostEstimate(
            flops=6 * rows * model * heads * HEAD_DIM, bytes_accessed=6 * model * heads * HEAD_DIM, transcendentals=0
        ),
    )(x, shift, scale, wq, wk, wv, qg[:, None, :], kg[:, None, :])


def attend_kernel(sources, parts, live_ref, *refs):
    q_refs = refs[: parts[0]]
    kv_refs = refs[parts[0] : parts[0] + sources * parts[1]]
    o_ref, max_ref, sum_ref, acc_ref = refs[parts[0] + sources * parts[1] :]
    q = jnp.concatenate([r[0] for r in q_refs], axis=0)
    part_rows = kv_refs[0].shape[2]
    block = part_rows * parts[1]

    def fold(s, first):
        mine = kv_refs[s * parts[1] : (s + 1) * parts[1]]
        live = live_ref[s]
        keys = jnp.concatenate([r[0, 0] for r in mine], axis=0)
        values = jnp.concatenate([r[1, 0] for r in mine], axis=0)
        scores = lax.dot_general(q, keys, (((1,), (1,)), ((), ())), preferred_element_type=jnp.float32)
        slot = lax.broadcasted_iota(jnp.int32, (1, block), 1)
        scores = jnp.where(slot < live, scores, NEG_FILL)
        top = jnp.max(scores, axis=1, keepdims=True)
        if not first:
            old = max_ref[:, :1]
            top = jnp.maximum(top, old)
            factor = jnp.exp2((old - top) * FACTOR)
        weights = jnp.exp2((scores - top) * FACTOR)
        total = weights[:, :HEAD_DIM]
        for i in range(1, block // HEAD_DIM):
            total += weights[:, i * HEAD_DIM : (i + 1) * HEAD_DIM]
        product = jnp.dot(weights.astype(jnp.bfloat16), values, preferred_element_type=jnp.float32)
        if first:
            sum_ref[...] = total
            acc_ref[...] = product
        else:
            sum_ref[...] = sum_ref[...] * factor + total
            acc_ref[...] = acc_ref[...] * factor + product
        max_ref[...] = jnp.broadcast_to(top, max_ref.shape)

    fold(0, True)
    for s in range(1, sources):
        pl.when(live_ref[s] > 0)(functools.partial(fold, s, False))
    o_ref[...] = (acc_ref[...] / jnp.sum(sum_ref[...], axis=1, keepdims=True)).astype(jnp.bfloat16)


def attend(live, queries, pieces):
    sources, key_parts = len(pieces), len(pieces[0])
    heads, part_rows, _ = queries[0].shape
    rows = part_rows * len(queries)
    q_spec = pl.BlockSpec((1, part_rows, HEAD_DIM), lambda h, live: (h, 0, 0))
    kv_spec = pl.BlockSpec((2, 1, pieces[0][0].shape[2], HEAD_DIM), lambda h, live: (0, h, 0, 0))
    flat = [p for piece in pieces for p in piece]
    keys = sources * key_parts * pieces[0][0].shape[2]
    return pl.pallas_call(
        functools.partial(attend_kernel, sources, (len(queries), key_parts)),
        grid_spec=pltpu.PrefetchScalarGridSpec(
            num_scalar_prefetch=1,
            grid=(heads,),
            in_specs=[q_spec] * len(queries) + [kv_spec] * len(flat),
            out_specs=pl.BlockSpec((rows, HEAD_DIM), lambda h, live: (0, h)),
            scratch_shapes=[pltpu.VMEM((rows, HEAD_DIM), jnp.float32)] * 3,
        ),
        out_shape=jax.ShapeDtypeStruct((rows, heads * HEAD_DIM), jnp.bfloat16),
        compiler_params=pltpu.CompilerParams(vmem_limit_bytes=VMEM_BYTES),
        cost_estimate=pl.CostEstimate(
            flops=4 * rows * keys * heads * HEAD_DIM,
            bytes_accessed=4 * keys * heads * HEAD_DIM,
            transcendentals=rows * keys * heads,
        ),
    )(live, *queries, *flat)


def on_device(
    latents,
    w_query,
    w_key,
    w_value,
    w_out,
    query_gain,
    key_gain,
    mod_table,
    levels,
    span_counts,
    block_mask,
    span_order,
):
    row_count, shard_width = latents.shape
    spans = lax.axis_size("frame")
    me = lax.axis_index("frame")
    column_start = lax.axis_index("tensor") * shard_width
    modulation = lax.dynamic_index_in_dim(mod_table, levels[0], 0, keepdims=False)
    shift_row, scale_row, gate_row = modulation[0:1], modulation[1:2], modulation[2]

    def from_ahead(block, distance):
        return lax.ppermute(block, "frame", [((i + distance) % spans, i) for i in range(spans)])

    part_rows = row_count // GATHER_PARTS
    queries, pieces = [], [[] for _ in range(spans)]
    for c in range(GATHER_PARTS):
        block = latents[c * part_rows : (c + 1) * part_rows]
        x = lax.all_gather(block, "tensor", axis=0)
        q, kv = qkv(x, shift_row, scale_row, w_query, w_key, w_value, query_gain, key_gain)
        queries.append(q)
        for s in range(spans):
            pieces[s].append(kv if s == 0 else None)
        for s in range(2, spans, 2):
            pieces[s][c] = from_ahead(kv, s)
        swapped = []
        for s in range(0, spans, 2):
            swapped.append(
                lax.ppermute(pieces[s][c], "frame", [(i ^ 1, i) for i in range(spans)])
            )
        for s in range(0, spans, 2):
            pieces[s + 1][c] = swapped[s // 2]

    offsets = jnp.arange(spans, dtype=jnp.int32)
    span_of = lax.rem(jnp.where(offsets % 2 == 0, me, me ^ 1) + offsets // 2 * 2, spans)
    own = offsets == 0
    allowed = (span_order[span_of] <= span_order[me]) & ((block_mask[0][span_of] == 1) | own)
    live = jnp.where(allowed, span_counts[span_of], 0).astype(jnp.int32)

    gate_part = lax.dynamic_slice_in_dim(gate_row, column_start, shard_width)
    per = GATHER_PARTS // QUERY_PARTS
    results = []
    for c in range(QUERY_PARTS):
        attended = attend(live, queries[c * per : (c + 1) * per], pieces)
        partial_out = jnp.dot(attended, w_out, preferred_element_type=jnp.float32).astype(jnp.bfloat16)
        projected = lax.psum_scatter(partial_out, "tensor", scatter_dimension=1, tiled=True).astype(jnp.float32)
        rows = latents[c * per * part_rows : (c + 1) * per * part_rows].astype(jnp.float32)
        results.append((rows + gate_part * projected).astype(jnp.bfloat16))
    return jnp.concatenate(results, axis=0)


def solution(mesh):
    return jax.shard_map(
        on_device,
        mesh=mesh,
        in_specs=(
            P("frame", "tensor"),
            P(None, "tensor"),
            P(None, "tensor"),
            P(None, "tensor"),
            P("tensor", None),
            P("tensor", None),
            P("tensor", None),
            P(),
            P("frame"),
            P(),
            P("frame", None),
            P(),
        ),
        out_specs=P("frame", "tensor"),
        check_vma=False,
    )
```

```python
import functools
import math

import jax
import jax.numpy as jnp
from jax import lax
from jax.experimental import pallas as pl
from jax.experimental.pallas import tpu as pltpu
from jax.sharding import PartitionSpec as P

HEAD_DIM = 128
EPSILON = 1e-06
NEG_FILL = -1e30
GATHER_PARTS = 4
QUERY_PARTS = 2
VMEM_BYTES = 56 * 1024 * 1024
FACTOR = math.log2(math.e) / math.sqrt(HEAD_DIM)


def gather_kernel(
    x_ref, shift_ref, scale_ref, wq_hbm, wk_hbm, wv_hbm, qg_ref, kg_ref,
    q_ref, kv_ref,
    w_ref, g_ref, normed_ref, own_ref,
    w_sem, right_send, right_recv, left_send, left_recv,
    peer_send, peer_recv, pair_send, pair_recv, local_sem,
):
    parts, shards, rows, width = g_ref.shape
    heads = q_ref.shape[1]
    model = shards * width
    spans = kv_ref.shape[0]
    pairs = spans // 2
    f, t = lax.axis_index("frame"), lax.axis_index("tensor")
    sibling = f + 1 - 2 * (f % 2)

    loads = [pltpu.make_async_copy(w, w_ref.at[i], w_sem.at[i]) for i, w in enumerate((wq_hbm, wk_hbm, wv_hbm))]
    for load in loads:
        load.start()

    barrier = pltpu.get_barrier_semaphore()

    def greet(device):
        pl.semaphore_signal(barrier, inc=1, device_id=device, device_id_type=pl.DeviceIdType.MESH)

    has_left, has_right = t > 0, t < shards - 1
    pl.when(has_left)(lambda: greet((f, t - 1)))
    pl.when(has_right)(lambda: greet((f, t + 1)))
    for k in range(1, pairs):
        greet(((f + 2 * k) % spans, t))
    greet((sibling, t))

    for c in range(parts):
        g_ref[c, t] = x_ref[c * rows : (c + 1) * rows]

    pl.semaphore_wait(barrier, pairs + jnp.where(has_left, 1, 0) + jnp.where(has_right, 1, 0))

    def remote(src, dst, send, recv, device):
        return pltpu.make_async_remote_copy(
            src_ref=src, dst_ref=dst, send_sem=send, recv_sem=recv,
            device_id=device, device_id_type=pl.DeviceIdType.MESH,
        )

    def go_right(c, d):
        block = g_ref.at[c, t - d]
        return remote(block, block, right_send.at[c, d], right_recv.at[c, d], (f, t + 1))

    def go_left(c, d):
        block = g_ref.at[c, t + d]
        return remote(block, block, left_send.at[c, d], left_recv.at[c, d], (f, t - 1))

    def come_right(c, d):
        block = g_ref.at[c, t - d]
        return remote(block, block, right_send.at[c, d - 1], right_recv.at[c, d - 1], (f, t - 1))

    def come_left(c, d):
        block = g_ref.at[c, t + d]
        return remote(block, block, left_send.at[c, d - 1], left_recv.at[c, d - 1], (f, t + 1))

    def to_peer(c, k):
        return remote(
            own_ref.at[c], kv_ref.at[2 * k, c], peer_send.at[c, k], peer_recv.at[c, k],
            ((f + spans - 2 * k) % spans, t),
        )

    def to_sibling(c, k):
        src = own_ref.at[c] if k == 0 else kv_ref.at[2 * k, c]
        return remote(src, kv_ref.at[2 * k + 1, c], pair_send.at[c, k], pair_recv.at[c, k], (sibling, t))

    def keep(c):
        return pltpu.make_async_copy(own_ref.at[c], kv_ref.at[0, c], local_sem.at[c])

    def send_own(c):
        pl.when(has_right)(lambda: go_right(c, 0).start())
        pl.when(has_left)(lambda: go_left(c, 0).start())

    def pass_on(c):
        for k in range(1, pairs):
            to_peer(c, k).wait_recv()
            to_sibling(c, k).start()

    ahead = min(2, parts)
    for c in range(ahead):
        send_own(c)

    def head_norm(shaped, gain):
        power = jnp.mean(shaped * shaped, axis=-1, keepdims=True)
        return (shaped * lax.rsqrt(power + EPSILON) * gain).astype(jnp.bfloat16)

    group = 2 if heads % 2 == 0 else 1
    span_width = group * HEAD_DIM

    def one_part(c, carried):
        for d in range(1, shards):

            @pl.when(t - d >= 0)
            def _():
                come_right(c, d).wait_recv()
                if d < shards - 1:
                    pl.when(has_right)(lambda: go_right(c, d).start())

            @pl.when(t + d < shards)
            def _():
                come_left(c, d).wait_recv()
                if d < shards - 1:
                    pl.when(has_left)(lambda: go_left(c, d).start())

        pl.when(c + ahead < parts)(lambda: send_own(c + ahead))

        total = jnp.zeros((rows, 1), jnp.float32)
        square = jnp.zeros((rows, 1), jnp.float32)
        for i in range(shards):
            x = g_ref[c, i].astype(jnp.float32)
            total += jnp.sum(x, axis=1, keepdims=True)
            square += jnp.sum(x * x, axis=1, keepdims=True)
        mean = total / model
        inverse = lax.rsqrt(square / model - mean * mean + EPSILON)
        for i in range(shards):
            columns = slice(i * width, (i + 1) * width)
            x = g_ref[c, i].astype(jnp.float32)
            y = (x - mean) * inverse * (1.0 + scale_ref[:, columns]) + shift_ref[:, columns]
            normed_ref[:, columns] = y.astype(jnp.bfloat16)

        @pl.when(c == 0)
        def _():
            for load in loads:
                load.wait()

        def one_group(j, carried):
            columns = pl.ds(pl.multiple_of(j * span_width, span_width), span_width)
            k, v, q = [
                jnp.dot(normed_ref[...], w_ref[i, :, columns], preferred_element_type=jnp.float32) for i in (1, 2, 0)
            ]
            for h in range(group):
                part = slice(h * HEAD_DIM, (h + 1) * HEAD_DIM)
                head = j * group + h
                own_ref[c, 0, head] = head_norm(k[:, part], kg_ref[head])
                own_ref[c, 1, head] = v[:, part].astype(jnp.bfloat16)
                q_ref[c, head] = head_norm(q[:, part], qg_ref[head])
            return carried

        lax.fori_loop(0, heads // group, one_group, 0)
        for k in range(1, pairs):
            to_peer(c, k).start()
        to_sibling(c, 0).start()
        keep(c).start()
        pl.when(c > 0)(lambda: pass_on(c - 1))
        return carried

    lax.fori_loop(0, parts, one_part, 0)
    pass_on(parts - 1)

    def finish(c, carried):
        for d in range(shards - 1):
            pl.when((t - d >= 0) & has_right)(lambda: go_right(c, d).wait_send())
            pl.when((t + d < shards) & has_left)(lambda: go_left(c, d).wait_send())
        for k in range(1, pairs):
            to_peer(c, k).wait_send()
        for k in range(pairs):
            to_sibling(c, k).wait()
        keep(c).wait()
        return carried

    lax.fori_loop(0, parts, finish, 0)


def gather_project(x, shift, scale, wq, wk, wv, qg, kg, parts):
    shards, spans = lax.axis_size("tensor"), lax.axis_size("frame")
    row_count, width = x.shape
    rows, model = row_count // parts, shards * width
    heads = wq.shape[1] // HEAD_DIM
    vmem = pl.BlockSpec(memory_space=pltpu.VMEM)
    hbm = pl.BlockSpec(memory_space=pl.ANY)
    dma = pltpu.SemaphoreType.DMA
    return pl.pallas_call(
        gather_kernel,
        in_specs=[vmem, vmem, vmem, hbm, hbm, hbm, vmem, vmem],
        out_specs=[vmem, hbm],
        out_shape=[
            jax.ShapeDtypeStruct((parts, heads, rows, HEAD_DIM), jnp.bfloat16),
            jax.ShapeDtypeStruct((spans, parts, 2, heads, rows, HEAD_DIM), jnp.bfloat16),
        ],
        scratch_shapes=[
            pltpu.VMEM((3, model, heads * HEAD_DIM), jnp.bfloat16),
            pltpu.VMEM((parts, shards, rows, width), jnp.bfloat16),
            pltpu.VMEM((rows, model), jnp.bfloat16),
            pltpu.VMEM((parts, 2, heads, rows, HEAD_DIM), jnp.bfloat16),
            dma((3,)),
        ]
        + [dma((parts, shards))] * 4
        + [dma((parts, spans // 2))] * 4
        + [dma((parts,))],
        compiler_params=pltpu.CompilerParams(vmem_limit_bytes=VMEM_BYTES, collective_id=0, has_side_effects=True),
        cost_estimate=pl.CostEstimate(
            flops=6 * row_count * model * heads * HEAD_DIM, bytes_accessed=6 * model * heads * HEAD_DIM, transcendentals=0
        ),
    )(x, shift, scale, wq, wk, wv, qg[:, None, :], kg[:, None, :])


def attend_kernel(live_ref, q_ref, kv_ref, o_ref, max_ref, sum_ref, acc_ref):
    sources, key_parts = kv_ref.shape[0], kv_ref.shape[1]
    q = jnp.concatenate([q_ref[i, 0] for i in range(q_ref.shape[0])], axis=0)
    block = kv_ref.shape[4] * key_parts

    def fold(s, first):
        live = live_ref[s]
        keys = jnp.concatenate([kv_ref[s, i, 0, 0] for i in range(key_parts)], axis=0)
        values = jnp.concatenate([kv_ref[s, i, 1, 0] for i in range(key_parts)], axis=0)
        scores = lax.dot_general(q, keys, (((1,), (1,)), ((), ())), preferred_element_type=jnp.float32)
        slot = lax.broadcasted_iota(jnp.int32, (1, block), 1)
        scores = jnp.where(slot < live, scores, NEG_FILL)
        top = jnp.max(scores, axis=1, keepdims=True)
        if not first:
            old = max_ref[:, :1]
            top = jnp.maximum(top, old)
            factor = jnp.exp2((old - top) * FACTOR)
        weights = jnp.exp2((scores - top) * FACTOR)
        total = weights[:, :HEAD_DIM]
        for i in range(1, block // HEAD_DIM):
            total += weights[:, i * HEAD_DIM : (i + 1) * HEAD_DIM]
        product = jnp.dot(weights.astype(jnp.bfloat16), values, preferred_element_type=jnp.float32)
        if first:
            sum_ref[...] = total
            acc_ref[...] = product
        else:
            sum_ref[...] = sum_ref[...] * factor + total
            acc_ref[...] = acc_ref[...] * factor + product
        max_ref[...] = jnp.broadcast_to(top, max_ref.shape)

    fold(0, True)
    for s in range(1, sources):
        pl.when(live_ref[s] > 0)(functools.partial(fold, s, False))
    o_ref[...] = (acc_ref[...] / jnp.sum(sum_ref[...], axis=1, keepdims=True)).astype(jnp.bfloat16)


def attend(live, queries, pieces, part, per):
    sources, key_parts, _, heads, part_rows, _ = pieces.shape
    rows = part_rows * per
    q_spec = pl.BlockSpec((per, 1, part_rows, HEAD_DIM), lambda h, live: (part, h, 0, 0))
    kv_spec = pl.BlockSpec((sources, key_parts, 2, 1, part_rows, HEAD_DIM), lambda h, live: (0, 0, 0, h, 0, 0))
    keys = sources * key_parts * part_rows
    return pl.pallas_call(
        attend_kernel,
        grid_spec=pltpu.PrefetchScalarGridSpec(
            num_scalar_prefetch=1,
            grid=(heads,),
            in_specs=[q_spec, kv_spec],
            out_specs=pl.BlockSpec((rows, HEAD_DIM), lambda h, live: (0, h)),
            scratch_shapes=[pltpu.VMEM((rows, HEAD_DIM), jnp.float32)] * 3,
        ),
        out_shape=jax.ShapeDtypeStruct((rows, heads * HEAD_DIM), jnp.bfloat16),
        compiler_params=pltpu.CompilerParams(vmem_limit_bytes=VMEM_BYTES),
        cost_estimate=pl.CostEstimate(
            flops=4 * rows * keys * heads * HEAD_DIM,
            bytes_accessed=4 * keys * heads * HEAD_DIM,
            transcendentals=rows * keys * heads,
        ),
    )(live, queries, pieces)


def on_device(
    latents,
    w_query,
    w_key,
    w_value,
    w_out,
    query_gain,
    key_gain,
    mod_table,
    levels,
    span_counts,
    block_mask,
    span_order,
):
    row_count, shard_width = latents.shape
    spans = lax.axis_size("frame")
    me = lax.axis_index("frame")
    column_start = lax.axis_index("tensor") * shard_width
    modulation = lax.dynamic_index_in_dim(mod_table, levels[0], 0, keepdims=False)
    shift_row, scale_row, gate_row = modulation[0:1], modulation[1:2], modulation[2]

    part_rows = row_count // GATHER_PARTS
    queries, pieces = gather_project(
        latents, shift_row, scale_row, w_query, w_key, w_value, query_gain, key_gain, GATHER_PARTS
    )

    offsets = jnp.arange(spans, dtype=jnp.int32)
    span_of = lax.rem(jnp.where(offsets % 2 == 0, me, me ^ 1) + offsets // 2 * 2, spans)
    own = offsets == 0
    allowed = (span_order[span_of] <= span_order[me]) & ((block_mask[0][span_of] == 1) | own)
    live = jnp.where(allowed, span_counts[span_of], 0).astype(jnp.int32)

    gate_part = lax.dynamic_slice_in_dim(gate_row, column_start, shard_width)
    per = GATHER_PARTS // QUERY_PARTS
    results = []
    for c in range(QUERY_PARTS):
        attended = attend(live, queries, pieces, c, per)
        partial_out = jnp.dot(attended, w_out, preferred_element_type=jnp.float32).astype(jnp.bfloat16)
        projected = lax.psum_scatter(partial_out, "tensor", scatter_dimension=1, tiled=True).astype(jnp.float32)
        rows = latents[c * per * part_rows : (c + 1) * per * part_rows].astype(jnp.float32)
        results.append((rows + gate_part * projected).astype(jnp.bfloat16))
    return jnp.concatenate(results, axis=0)


def solution(mesh):
    return jax.shard_map(
        on_device,
        mesh=mesh,
        in_specs=(
            P("frame", "tensor"),
            P(None, "tensor"),
            P(None, "tensor"),
            P(None, "tensor"),
            P("tensor", None),
            P("tensor", None),
            P("tensor", None),
            P(),
            P("frame"),
            P(),
            P("frame", None),
            P(),
        ),
        out_specs=P("frame", "tensor"),
        check_vma=False,
    )
```

```python
import math

import jax
import jax.numpy as jnp
from jax import lax
from jax.experimental import pallas as pl
from jax.experimental.pallas import tpu as pltpu
from jax.sharding import PartitionSpec as P

HEAD_DIM = 128
EPSILON = 1e-06
NEG_FILL = -1e30
GATHER_PARTS = 4
VMEM_BYTES = 56 * 1024 * 1024
FACTOR = math.log2(math.e) / math.sqrt(HEAD_DIM)


def gather_kernel(
    x_ref, shift_ref, scale_ref, wq_hbm, wk_hbm, wv_hbm, qg_ref, kg_ref,
    q_ref, kv_ref,
    w_ref, g_ref, normed_ref, own_ref,
    w_sem, right_send, right_recv, left_send, left_recv,
    peer_send, peer_recv, pair_send, pair_recv, local_sem,
):
    parts, shards, rows, width = g_ref.shape
    heads = q_ref.shape[1]
    model = shards * width
    spans = kv_ref.shape[0]
    pairs = spans // 2
    f, t = lax.axis_index("frame"), lax.axis_index("tensor")
    sibling = f + 1 - 2 * (f % 2)

    loads = [pltpu.make_async_copy(w, w_ref.at[i], w_sem.at[i]) for i, w in enumerate((wq_hbm, wk_hbm, wv_hbm))]
    for load in loads:
        load.start()

    barrier = pltpu.get_barrier_semaphore()

    def greet(device):
        pl.semaphore_signal(barrier, inc=1, device_id=device, device_id_type=pl.DeviceIdType.MESH)

    has_left, has_right = t > 0, t < shards - 1
    pl.when(has_left)(lambda: greet((f, t - 1)))
    pl.when(has_right)(lambda: greet((f, t + 1)))
    for k in range(1, pairs):
        greet(((f + 2 * k) % spans, t))
    greet((sibling, t))

    for c in range(parts):
        g_ref[c, t] = x_ref[c * rows : (c + 1) * rows]

    pl.semaphore_wait(barrier, pairs + jnp.where(has_left, 1, 0) + jnp.where(has_right, 1, 0))

    def remote(src, dst, send, recv, device):
        return pltpu.make_async_remote_copy(
            src_ref=src, dst_ref=dst, send_sem=send, recv_sem=recv,
            device_id=device, device_id_type=pl.DeviceIdType.MESH,
        )

    def go_right(c, d):
        block = g_ref.at[c, t - d]
        return remote(block, block, right_send.at[c, d], right_recv.at[c, d], (f, t + 1))

    def go_left(c, d):
        block = g_ref.at[c, t + d]
        return remote(block, block, left_send.at[c, d], left_recv.at[c, d], (f, t - 1))

    def come_right(c, d):
        block = g_ref.at[c, t - d]
        return remote(block, block, right_send.at[c, d - 1], right_recv.at[c, d - 1], (f, t - 1))

    def come_left(c, d):
        block = g_ref.at[c, t + d]
        return remote(block, block, left_send.at[c, d - 1], left_recv.at[c, d - 1], (f, t + 1))

    def to_peer(c, k):
        return remote(
            own_ref.at[c], kv_ref.at[2 * k, c], peer_send.at[c, k], peer_recv.at[c, k],
            ((f + spans - 2 * k) % spans, t),
        )

    def to_sibling(c, k):
        src = own_ref.at[c] if k == 0 else kv_ref.at[2 * k, c]
        return remote(src, kv_ref.at[2 * k + 1, c], pair_send.at[c, k], pair_recv.at[c, k], (sibling, t))

    def keep(c):
        return pltpu.make_async_copy(own_ref.at[c], kv_ref.at[0, c], local_sem.at[c])

    def send_own(c):
        pl.when(has_right)(lambda: go_right(c, 0).start())
        pl.when(has_left)(lambda: go_left(c, 0).start())

    def pass_on(c):
        for k in range(1, pairs):
            to_peer(c, k).wait_recv()
            to_sibling(c, k).start()

    ahead = min(2, parts)
    for c in range(ahead):
        send_own(c)

    def head_norm(shaped, gain):
        power = jnp.mean(shaped * shaped, axis=-1, keepdims=True)
        return (shaped * lax.rsqrt(power + EPSILON) * gain).astype(jnp.bfloat16)

    group = 2 if heads % 2 == 0 else 1
    span_width = group * HEAD_DIM

    def one_part(c, carried):
        for d in range(1, shards):

            @pl.when(t - d >= 0)
            def _():
                come_right(c, d).wait_recv()
                if d < shards - 1:
                    pl.when(has_right)(lambda: go_right(c, d).start())

            @pl.when(t + d < shards)
            def _():
                come_left(c, d).wait_recv()
                if d < shards - 1:
                    pl.when(has_left)(lambda: go_left(c, d).start())

        pl.when(c + ahead < parts)(lambda: send_own(c + ahead))

        total = jnp.zeros((rows, 1), jnp.float32)
        square = jnp.zeros((rows, 1), jnp.float32)
        for i in range(shards):
            x = g_ref[c, i].astype(jnp.float32)
            total += jnp.sum(x, axis=1, keepdims=True)
            square += jnp.sum(x * x, axis=1, keepdims=True)
        mean = total / model
        inverse = lax.rsqrt(square / model - mean * mean + EPSILON)
        for i in range(shards):
            columns = slice(i * width, (i + 1) * width)
            x = g_ref[c, i].astype(jnp.float32)
            y = (x - mean) * inverse * (1.0 + scale_ref[:, columns]) + shift_ref[:, columns]
            normed_ref[:, columns] = y.astype(jnp.bfloat16)

        @pl.when(c == 0)
        def _():
            for load in loads:
                load.wait()

        def one_group(j, carried):
            columns = pl.ds(pl.multiple_of(j * span_width, span_width), span_width)
            k, v, q = [
                jnp.dot(normed_ref[...], w_ref[i, :, columns], preferred_element_type=jnp.float32) for i in (1, 2, 0)
            ]
            for h in range(group):
                part = slice(h * HEAD_DIM, (h + 1) * HEAD_DIM)
                head = j * group + h
                own_ref[c, 0, head] = head_norm(k[:, part], kg_ref[head])
                own_ref[c, 1, head] = v[:, part].astype(jnp.bfloat16)
                q_ref[c, head] = head_norm(q[:, part], qg_ref[head])
            return carried

        lax.fori_loop(0, heads // group, one_group, 0)
        for k in range(1, pairs):
            to_peer(c, k).start()
        to_sibling(c, 0).start()
        keep(c).start()
        pl.when(c > 0)(lambda: pass_on(c - 1))
        return carried

    lax.fori_loop(0, parts, one_part, 0)
    pass_on(parts - 1)

    def finish(c, carried):
        for d in range(shards - 1):
            pl.when((t - d >= 0) & has_right)(lambda: go_right(c, d).wait_send())
            pl.when((t + d < shards) & has_left)(lambda: go_left(c, d).wait_send())
        for k in range(1, pairs):
            to_peer(c, k).wait_send()
        for k in range(pairs):
            to_sibling(c, k).wait()
        keep(c).wait()
        return carried

    lax.fori_loop(0, parts, finish, 0)


def gather_project(x, shift, scale, wq, wk, wv, qg, kg, parts):
    shards, spans = lax.axis_size("tensor"), lax.axis_size("frame")
    row_count, width = x.shape
    rows, model = row_count // parts, shards * width
    heads = wq.shape[1] // HEAD_DIM
    vmem = pl.BlockSpec(memory_space=pltpu.VMEM)
    hbm = pl.BlockSpec(memory_space=pl.ANY)
    dma = pltpu.SemaphoreType.DMA
    return pl.pallas_call(
        gather_kernel,
        in_specs=[vmem, vmem, vmem, hbm, hbm, hbm, vmem, vmem],
        out_specs=[vmem, hbm],
        out_shape=[
            jax.ShapeDtypeStruct((parts, heads, rows, HEAD_DIM), jnp.bfloat16),
            jax.ShapeDtypeStruct((spans, parts, 2, heads, rows, HEAD_DIM), jnp.bfloat16),
        ],
        scratch_shapes=[
            pltpu.VMEM((3, model, heads * HEAD_DIM), jnp.bfloat16),
            pltpu.VMEM((parts, shards, rows, width), jnp.bfloat16),
            pltpu.VMEM((rows, model), jnp.bfloat16),
            pltpu.VMEM((parts, 2, heads, rows, HEAD_DIM), jnp.bfloat16),
            dma((3,)),
        ]
        + [dma((parts, shards))] * 4
        + [dma((parts, spans // 2))] * 4
        + [dma((parts,))],
        compiler_params=pltpu.CompilerParams(vmem_limit_bytes=VMEM_BYTES, collective_id=0, has_side_effects=True),
        cost_estimate=pl.CostEstimate(
            flops=6 * row_count * model * heads * HEAD_DIM, bytes_accessed=6 * model * heads * HEAD_DIM, transcendentals=0
        ),
    )(x, shift, scale, wq, wk, wv, qg[:, None, :], kg[:, None, :])


def attend_kernel(
    live_ref, q_ref, kv_hbm, wo_hbm, x_ref, gate_ref,
    o_ref,
    kv_ref, wo_ref, attended_ref, part_ref, right_ref, left_ref, total_ref,
    kv_sem, wo_sem, right_send, right_recv, left_send, left_recv,
):
    heads, sources, parts, _, rows, _ = kv_ref.shape
    shards, width = part_ref.shape[1], part_ref.shape[3]
    block = parts * rows
    f, t = lax.axis_index("frame"), lax.axis_index("tensor")
    has_left, has_right = t > 0, t < shards - 1

    def load(h):
        return pltpu.make_async_copy(kv_hbm.at[:, :, :, h], kv_ref.at[h], kv_sem.at[h])

    for h in range(heads):
        load(h).start()
    load_out = pltpu.make_async_copy(wo_hbm, wo_ref, wo_sem)
    load_out.start()

    barrier = pltpu.get_barrier_semaphore()

    def greet(device):
        pl.semaphore_signal(barrier, inc=1, device_id=device, device_id_type=pl.DeviceIdType.MESH)

    pl.when(has_left)(lambda: greet((f, t - 1)))
    pl.when(has_right)(lambda: greet((f, t + 1)))
    pl.semaphore_wait(barrier, jnp.where(has_left, 1, 0) + jnp.where(has_right, 1, 0))

    def right(c, j, src):
        return pltpu.make_async_remote_copy(
            src_ref=src.at[c, j], dst_ref=right_ref.at[c, j], send_sem=right_send.at[c, j], recv_sem=right_recv.at[c, j],
            device_id=(f, t + 1), device_id_type=pl.DeviceIdType.MESH,
        )

    def left(c, j, src):
        return pltpu.make_async_remote_copy(
            src_ref=src.at[c, j], dst_ref=left_ref.at[c, j], send_sem=left_send.at[c, j], recv_sem=left_recv.at[c, j],
            device_id=(f, t - 1), device_id_type=pl.DeviceIdType.MESH,
        )

    def begin(c):
        @pl.when(t == 0)
        def _():
            for j in range(shards - 1, 0, -1):
                right(c, j, part_ref).start()

        @pl.when(t == shards - 1)
        def _():
            for j in range(shards - 1):
                left(c, j, part_ref).start()

    def relay(c):
        for e in range(shards - 1, 0, -1):

            @pl.when(has_left & (t + e < shards))
            def _():
                j = t + e
                right(c, j, right_ref).wait_recv()
                both = right_ref[c, j].astype(jnp.float32) + part_ref[c, j].astype(jnp.float32)
                right_ref[c, j] = both.astype(jnp.bfloat16)
                right(c, j, right_ref).start()

            @pl.when(has_right & (t - e >= 0))
            def _():
                j = t - e
                left(c, j, left_ref).wait_recv()
                both = left_ref[c, j].astype(jnp.float32) + part_ref[c, j].astype(jnp.float32)
                left_ref[c, j] = both.astype(jnp.bfloat16)
                left(c, j, left_ref).start()

    def one_part(c, carried):
        def one_head(h, carried):
            pl.when(c == 0)(lambda: load(h).wait())
            q = q_ref[c, h]
            for s in range(sources):
                keys = jnp.concatenate([kv_ref[h, s, i, 0] for i in range(parts)], axis=0)
                values = jnp.concatenate([kv_ref[h, s, i, 1] for i in range(parts)], axis=0)
                scores = lax.dot_general(q, keys, (((1,), (1,)), ((), ())), preferred_element_type=jnp.float32)
                slot = lax.broadcasted_iota(jnp.int32, (1, block), 1)
                scores = jnp.where(slot < live_ref[s], scores, NEG_FILL)
                top = jnp.max(scores, axis=1, keepdims=True)
                if s > 0:
                    top = jnp.maximum(top, best)
                    factor = jnp.exp2((best - top) * FACTOR)
                best = top
                weights = jnp.exp2((scores - top) * FACTOR)
                total = weights[:, :HEAD_DIM]
                for i in range(1, block // HEAD_DIM):
                    total += weights[:, i * HEAD_DIM : (i + 1) * HEAD_DIM]
                product = jnp.dot(weights.astype(jnp.bfloat16), values, preferred_element_type=jnp.float32)
                if s == 0:
                    summed, accum = total, product
                else:
                    summed, accum = summed * factor + total, accum * factor + product
            result = accum / jnp.sum(summed, axis=1, keepdims=True)
            attended_ref[h] = result.astype(jnp.bfloat16)
            return carried

        lax.fori_loop(0, heads, one_head, 0)
        pl.when(c == 0)(lambda: load_out.wait())
        attended = jnp.concatenate([attended_ref[h] for h in range(heads)], axis=1)
        for j in range(shards):
            term = jnp.dot(attended, wo_ref[:, j * width : (j + 1) * width], preferred_element_type=jnp.float32)
            part_ref[c, j] = term.astype(jnp.bfloat16)
        begin(c)
        pl.when(c > 0)(lambda: relay(c - 1))
        return carried

    lax.fori_loop(0, parts, one_part, 0)
    relay(parts - 1)

    def finish(c, carried):
        total_ref[...] = part_ref[c, t].astype(jnp.float32)

        @pl.when(has_left)
        def _():
            right(c, t, right_ref).wait_recv()
            total_ref[...] += right_ref[c, t].astype(jnp.float32)

        @pl.when(has_right)
        def _():
            left(c, t, left_ref).wait_recv()
            total_ref[...] += left_ref[c, t].astype(jnp.float32)

        here = pl.ds(pl.multiple_of(c * rows, rows), rows)
        updated = x_ref[here, :].astype(jnp.float32) + gate_ref[...] * total_ref[...]
        o_ref[here, :] = updated.astype(jnp.bfloat16)
        for e in range(1, shards):
            pl.when(t + e < shards)(lambda: right(c, t + e, right_ref).wait_send())
            pl.when(t - e >= 0)(lambda: left(c, t - e, left_ref).wait_send())
        return carried

    lax.fori_loop(0, parts, finish, 0)


def attend_project(live, queries, pieces, wo, x, gate):
    sources, parts, _, heads, rows, _ = pieces.shape
    shards, width = lax.axis_size("tensor"), x.shape[1]
    vmem = pl.BlockSpec(memory_space=pltpu.VMEM)
    hbm = pl.BlockSpec(memory_space=pl.ANY)
    dma = pltpu.SemaphoreType.DMA
    keys = sources * parts * rows
    return pl.pallas_call(
        attend_kernel,
        in_specs=[pl.BlockSpec(memory_space=pltpu.SMEM), vmem, hbm, hbm, vmem, vmem],
        out_specs=vmem,
        out_shape=jax.ShapeDtypeStruct(x.shape, jnp.bfloat16),
        scratch_shapes=[
            pltpu.VMEM((heads, sources, parts, 2, rows, HEAD_DIM), jnp.bfloat16),
            pltpu.VMEM(wo.shape, jnp.bfloat16),
            pltpu.VMEM((heads, rows, HEAD_DIM), jnp.bfloat16),
        ]
        + [pltpu.VMEM((parts, shards, rows, width), jnp.bfloat16)] * 3
        + [pltpu.VMEM((rows, width), jnp.float32), dma((heads,)), dma]
        + [dma((parts, shards))] * 4,
        compiler_params=pltpu.CompilerParams(vmem_limit_bytes=VMEM_BYTES, collective_id=1, has_side_effects=True),
        cost_estimate=pl.CostEstimate(
            flops=4 * x.shape[0] * keys * heads * HEAD_DIM,
            bytes_accessed=4 * keys * heads * HEAD_DIM,
            transcendentals=x.shape[0] * keys * heads,
        ),
    )(live, queries, pieces, wo, x, gate)


def on_device(
    latents,
    w_query,
    w_key,
    w_value,
    w_out,
    query_gain,
    key_gain,
    mod_table,
    levels,
    span_counts,
    block_mask,
    span_order,
):
    shard_width = latents.shape[1]
    spans = lax.axis_size("frame")
    me = lax.axis_index("frame")
    column_start = lax.axis_index("tensor") * shard_width
    modulation = lax.dynamic_index_in_dim(mod_table, levels[0], 0, keepdims=False)
    shift_row, scale_row, gate_row = modulation[0:1], modulation[1:2], modulation[2:3]

    queries, pieces = gather_project(
        latents, shift_row, scale_row, w_query, w_key, w_value, query_gain, key_gain, GATHER_PARTS
    )

    offsets = jnp.arange(spans, dtype=jnp.int32)
    span_of = lax.rem(jnp.where(offsets % 2 == 0, me, me ^ 1) + offsets // 2 * 2, spans)
    own = offsets == 0
    allowed = (span_order[span_of] <= span_order[me]) & ((block_mask[0][span_of] == 1) | own)
    live = jnp.where(allowed, span_counts[span_of], 0).astype(jnp.int32)

    gate_part = lax.dynamic_slice_in_dim(gate_row, column_start, shard_width, axis=1)
    return attend_project(live, queries, pieces, w_out, latents, gate_part)


def solution(mesh):
    return jax.shard_map(
        on_device,
        mesh=mesh,
        in_specs=(
            P("frame", "tensor"),
            P(None, "tensor"),
            P(None, "tensor"),
            P(None, "tensor"),
            P("tensor", None),
            P("tensor", None),
            P("tensor", None),
            P(),
            P("frame"),
            P(),
            P("frame", None),
            P(),
        ),
        out_specs=P("frame", "tensor"),
        check_vma=False,
    )
```

```python
import math

import jax
import jax.numpy as jnp
from jax import lax
from jax.experimental import pallas as pl
from jax.experimental.pallas import tpu as pltpu
from jax.sharding import PartitionSpec as P

HEAD_DIM = 128
EPSILON = 1e-06
NEG_FILL = -1e30
GATHER_PARTS = 4
VMEM_BYTES = 56 * 1024 * 1024
FACTOR = math.log2(math.e) / math.sqrt(HEAD_DIM)


def gather_kernel(
    level_ref, x_ref, mod_ref, wq_hbm, wk_hbm, wv_hbm, qg_ref, kg_ref,
    q_ref, kv_ref,
    w_ref, g_ref, normed_ref, own_ref,
    w_sem, right_send, right_recv, left_send, left_recv,
    peer_send, peer_recv, pair_send, pair_recv, local_sem,
):
    parts, shards, rows, width = g_ref.shape
    heads = q_ref.shape[1]
    model = shards * width
    spans = kv_ref.shape[0]
    level = level_ref[0]
    pairs = spans // 2
    f, t = lax.axis_index("frame"), lax.axis_index("tensor")
    sibling = f + 1 - 2 * (f % 2)

    loads = [pltpu.make_async_copy(w, w_ref.at[i], w_sem.at[i]) for i, w in enumerate((wq_hbm, wk_hbm, wv_hbm))]
    for load in loads:
        load.start()

    barrier = pltpu.get_barrier_semaphore()

    def greet(device):
        pl.semaphore_signal(barrier, inc=1, device_id=device, device_id_type=pl.DeviceIdType.MESH)

    has_left, has_right = t > 0, t < shards - 1
    pl.when(has_left)(lambda: greet((f, t - 1)))
    pl.when(has_right)(lambda: greet((f, t + 1)))
    for k in range(1, pairs):
        greet(((f + 2 * k) % spans, t))
    greet((sibling, t))

    for c in range(parts):
        g_ref[c, t] = x_ref[c * rows : (c + 1) * rows]

    pl.semaphore_wait(barrier, pairs + jnp.where(has_left, 1, 0) + jnp.where(has_right, 1, 0))

    def remote(src, dst, send, recv, device):
        return pltpu.make_async_remote_copy(
            src_ref=src, dst_ref=dst, send_sem=send, recv_sem=recv,
            device_id=device, device_id_type=pl.DeviceIdType.MESH,
        )

    def go_right(c, d):
        block = g_ref.at[c, t - d]
        return remote(block, block, right_send.at[c, d], right_recv.at[c, d], (f, t + 1))

    def go_left(c, d):
        block = g_ref.at[c, t + d]
        return remote(block, block, left_send.at[c, d], left_recv.at[c, d], (f, t - 1))

    def come_right(c, d):
        block = g_ref.at[c, t - d]
        return remote(block, block, right_send.at[c, d - 1], right_recv.at[c, d - 1], (f, t - 1))

    def come_left(c, d):
        block = g_ref.at[c, t + d]
        return remote(block, block, left_send.at[c, d - 1], left_recv.at[c, d - 1], (f, t + 1))

    def to_peer(c, k):
        return remote(
            own_ref.at[c], kv_ref.at[2 * k, c], peer_send.at[c, k], peer_recv.at[c, k],
            ((f + spans - 2 * k) % spans, t),
        )

    def to_sibling(c, k):
        src = own_ref.at[c] if k == 0 else kv_ref.at[2 * k, c]
        return remote(src, kv_ref.at[2 * k + 1, c], pair_send.at[c, k], pair_recv.at[c, k], (sibling, t))

    def keep(c):
        return pltpu.make_async_copy(own_ref.at[c], kv_ref.at[0, c], local_sem.at[c])

    def send_own(c):
        pl.when(has_right)(lambda: go_right(c, 0).start())
        pl.when(has_left)(lambda: go_left(c, 0).start())

    def pass_on(c):
        for k in range(1, pairs):
            to_peer(c, k).wait_recv()
            to_sibling(c, k).start()

    ahead = min(2, parts)
    for c in range(ahead):
        send_own(c)

    def head_norm(shaped, gain):
        power = jnp.mean(shaped * shaped, axis=-1, keepdims=True)
        return (shaped * lax.rsqrt(power + EPSILON) * gain).astype(jnp.bfloat16)

    group = 2 if heads % 2 == 0 else 1
    span_width = group * HEAD_DIM

    def one_part(c, carried):
        for d in range(1, shards):

            @pl.when(t - d >= 0)
            def _():
                come_right(c, d).wait_recv()
                if d < shards - 1:
                    pl.when(has_right)(lambda: go_right(c, d).start())

            @pl.when(t + d < shards)
            def _():
                come_left(c, d).wait_recv()
                if d < shards - 1:
                    pl.when(has_left)(lambda: go_left(c, d).start())

        pl.when(c + ahead < parts)(lambda: send_own(c + ahead))

        total = jnp.zeros((rows, 1), jnp.float32)
        square = jnp.zeros((rows, 1), jnp.float32)
        for i in range(shards):
            x = g_ref[c, i].astype(jnp.float32)
            total += jnp.sum(x, axis=1, keepdims=True)
            square += jnp.sum(x * x, axis=1, keepdims=True)
        mean = total / model
        inverse = lax.rsqrt(square / model - mean * mean + EPSILON)
        for i in range(shards):
            columns = slice(i * width, (i + 1) * width)
            x = g_ref[c, i].astype(jnp.float32)
            y = (x - mean) * inverse * (1.0 + mod_ref[1, pl.ds(level, 1), columns]) + mod_ref[0, pl.ds(level, 1), columns]
            normed_ref[:, columns] = y.astype(jnp.bfloat16)

        @pl.when(c == 0)
        def _():
            for load in loads:
                load.wait()

        def product(i, j):
            columns = pl.ds(pl.multiple_of(j * span_width, span_width), span_width)
            return jnp.dot(normed_ref[...], w_ref[i, :, columns], preferred_element_type=jnp.float32)

        def keys_values(j, carried):
            k, v = product(1, j), product(2, j)
            for h in range(group):
                part = slice(h * HEAD_DIM, (h + 1) * HEAD_DIM)
                head = j * group + h
                own_ref[c, 0, head] = head_norm(k[:, part], kg_ref[pl.ds(head, 1), :])
                own_ref[c, 1, head] = v[:, part].astype(jnp.bfloat16)
            return carried

        def queries(j, carried):
            q = product(0, j)
            for h in range(group):
                part = slice(h * HEAD_DIM, (h + 1) * HEAD_DIM)
                head = j * group + h
                q_ref[c, head] = head_norm(q[:, part], qg_ref[pl.ds(head, 1), :])
            return carried

        lax.fori_loop(0, heads // group, keys_values, 0)
        for k in range(1, pairs):
            to_peer(c, k).start()
        to_sibling(c, 0).start()
        keep(c).start()
        lax.fori_loop(0, heads // group, queries, 0)
        pl.when(c > 0)(lambda: pass_on(c - 1))
        return carried

    lax.fori_loop(0, parts, one_part, 0)
    pass_on(parts - 1)

    def finish(c, carried):
        for d in range(shards - 1):
            pl.when((t - d >= 0) & has_right)(lambda: go_right(c, d).wait_send())
            pl.when((t + d < shards) & has_left)(lambda: go_left(c, d).wait_send())
        for k in range(1, pairs):
            to_peer(c, k).wait_send()
        for k in range(pairs):
            to_sibling(c, k).wait()
        keep(c).wait()
        return carried

    lax.fori_loop(0, parts, finish, 0)


def gather_project(level, x, mod, wq, wk, wv, qg, kg, parts):
    shards, spans = lax.axis_size("tensor"), lax.axis_size("frame")
    row_count, width = x.shape
    rows, model = row_count // parts, shards * width
    heads = wq.shape[1] // HEAD_DIM
    vmem = pl.BlockSpec(memory_space=pltpu.VMEM)
    hbm = pl.BlockSpec(memory_space=pl.ANY)
    dma = pltpu.SemaphoreType.DMA
    return pl.pallas_call(
        gather_kernel,
        in_specs=[pl.BlockSpec(memory_space=pltpu.SMEM), vmem, vmem, hbm, hbm, hbm, vmem, vmem],
        out_specs=[vmem, hbm],
        out_shape=[
            jax.ShapeDtypeStruct((parts, heads, rows, HEAD_DIM), jnp.bfloat16),
            jax.ShapeDtypeStruct((spans, parts, 2, heads, rows, HEAD_DIM), jnp.bfloat16),
        ],
        scratch_shapes=[
            pltpu.VMEM((3, model, heads * HEAD_DIM), jnp.bfloat16),
            pltpu.VMEM((parts, shards, rows, width), jnp.bfloat16),
            pltpu.VMEM((rows, model), jnp.bfloat16),
            pltpu.VMEM((parts, 2, heads, rows, HEAD_DIM), jnp.bfloat16),
            dma((3,)),
        ]
        + [dma((parts, shards))] * 4
        + [dma((parts, spans // 2))] * 4
        + [dma((parts,))],
        compiler_params=pltpu.CompilerParams(vmem_limit_bytes=VMEM_BYTES, collective_id=0, has_side_effects=True),
        cost_estimate=pl.CostEstimate(
            flops=6 * row_count * model * heads * HEAD_DIM, bytes_accessed=6 * model * heads * HEAD_DIM, transcendentals=0
        ),
    )(level, x, mod, wq, wk, wv, qg, kg)


def attend_kernel(
    level_ref, counts_ref, mask_ref, order_ref, q_ref, kv_hbm, wo_hbm, x_ref, mod_ref,
    o_ref,
    kv_ref, wo_ref, attended_ref, part_ref, right_ref, left_ref, total_ref,
    kv_sem, wo_sem, right_send, right_recv, left_send, left_recv,
):
    heads, sources, parts, _, rows, _ = kv_ref.shape
    shards, width = part_ref.shape[1], part_ref.shape[3]
    block = parts * rows
    f, t = lax.axis_index("frame"), lax.axis_index("tensor")
    has_left, has_right = t > 0, t < shards - 1

    live = []
    for s in range(sources):
        base = f if s % 2 == 0 else f + 1 - 2 * (f % 2)
        span = (base + s // 2 * 2) % sources
        allowed = order_ref[span] <= order_ref[f]
        if s > 0:
            allowed = allowed & (mask_ref[0, span] == 1)
        live.append(jnp.where(allowed, counts_ref[span], 0))

    def load(h):
        return pltpu.make_async_copy(kv_hbm.at[:, :, :, h], kv_ref.at[h], kv_sem.at[h])

    for h in range(heads):
        load(h).start()
    load_out = pltpu.make_async_copy(wo_hbm, wo_ref, wo_sem)
    load_out.start()

    barrier = pltpu.get_barrier_semaphore()

    def greet(device):
        pl.semaphore_signal(barrier, inc=1, device_id=device, device_id_type=pl.DeviceIdType.MESH)

    pl.when(has_left)(lambda: greet((f, t - 1)))
    pl.when(has_right)(lambda: greet((f, t + 1)))
    pl.semaphore_wait(barrier, jnp.where(has_left, 1, 0) + jnp.where(has_right, 1, 0))

    def right(c, j, src):
        return pltpu.make_async_remote_copy(
            src_ref=src.at[c, j], dst_ref=right_ref.at[c, j], send_sem=right_send.at[c, j], recv_sem=right_recv.at[c, j],
            device_id=(f, t + 1), device_id_type=pl.DeviceIdType.MESH,
        )

    def left(c, j, src):
        return pltpu.make_async_remote_copy(
            src_ref=src.at[c, j], dst_ref=left_ref.at[c, j], send_sem=left_send.at[c, j], recv_sem=left_recv.at[c, j],
            device_id=(f, t - 1), device_id_type=pl.DeviceIdType.MESH,
        )

    def begin(c):
        @pl.when(t == 0)
        def _():
            for j in range(shards - 1, 0, -1):
                right(c, j, part_ref).start()

        @pl.when(t == shards - 1)
        def _():
            for j in range(shards - 1):
                left(c, j, part_ref).start()

    def relay(c):
        for e in range(shards - 1, 0, -1):

            @pl.when(has_left & (t + e < shards))
            def _():
                j = t + e
                right(c, j, right_ref).wait_recv()
                both = right_ref[c, j].astype(jnp.float32) + part_ref[c, j].astype(jnp.float32)
                right_ref[c, j] = both.astype(jnp.bfloat16)
                right(c, j, right_ref).start()

            @pl.when(has_right & (t - e >= 0))
            def _():
                j = t - e
                left(c, j, left_ref).wait_recv()
                both = left_ref[c, j].astype(jnp.float32) + part_ref[c, j].astype(jnp.float32)
                left_ref[c, j] = both.astype(jnp.bfloat16)
                left(c, j, left_ref).start()

    def one_part(c, carried):
        def one_head(h, carried):
            pl.when(c == 0)(lambda: load(h).wait())
            q = q_ref[c, h]
            for s in range(sources):
                keys = jnp.concatenate([kv_ref[h, s, i, 0] for i in range(parts)], axis=0)
                values = jnp.concatenate([kv_ref[h, s, i, 1] for i in range(parts)], axis=0)
                scores = lax.dot_general(q, keys, (((1,), (1,)), ((), ())), preferred_element_type=jnp.float32)
                slot = lax.broadcasted_iota(jnp.int32, (1, block), 1)
                scores = jnp.where(slot < live[s], scores, NEG_FILL)
                top = jnp.max(scores, axis=1, keepdims=True)
                if s > 0:
                    top = jnp.maximum(top, best)
                    factor = jnp.exp2((best - top) * FACTOR)
                best = top
                weights = jnp.exp2((scores - top) * FACTOR)
                total = weights[:, :HEAD_DIM]
                for i in range(1, block // HEAD_DIM):
                    total += weights[:, i * HEAD_DIM : (i + 1) * HEAD_DIM]
                product = jnp.dot(weights.astype(jnp.bfloat16), values, preferred_element_type=jnp.float32)
                if s == 0:
                    summed, accum = total, product
                else:
                    summed, accum = summed * factor + total, accum * factor + product
            result = accum / jnp.sum(summed, axis=1, keepdims=True)
            attended_ref[h] = result.astype(jnp.bfloat16)
            return carried

        lax.fori_loop(0, heads, one_head, 0)
        pl.when(c == 0)(lambda: load_out.wait())
        attended = jnp.concatenate([attended_ref[h] for h in range(heads)], axis=1)
        for j in range(shards):
            term = jnp.dot(attended, wo_ref[:, j * width : (j + 1) * width], preferred_element_type=jnp.float32)
            part_ref[c, j] = term.astype(jnp.bfloat16)
        begin(c)
        pl.when(c > 0)(lambda: relay(c - 1))
        return carried

    lax.fori_loop(0, parts, one_part, 0)
    relay(parts - 1)

    def finish(c, carried):
        total_ref[...] = part_ref[c, t].astype(jnp.float32)

        @pl.when(has_left)
        def _():
            right(c, t, right_ref).wait_recv()
            total_ref[...] += right_ref[c, t].astype(jnp.float32)

        @pl.when(has_right)
        def _():
            left(c, t, left_ref).wait_recv()
            total_ref[...] += left_ref[c, t].astype(jnp.float32)

        here = pl.ds(pl.multiple_of(c * rows, rows), rows)
        gate = mod_ref[2, pl.ds(level_ref[0], 1), pl.ds(pl.multiple_of(t * width, width), width)]
        updated = x_ref[here, :].astype(jnp.float32) + gate * total_ref[...]
        o_ref[here, :] = updated.astype(jnp.bfloat16)
        for e in range(1, shards):
            pl.when(t + e < shards)(lambda: right(c, t + e, right_ref).wait_send())
            pl.when(t - e >= 0)(lambda: left(c, t - e, left_ref).wait_send())
        return carried

    lax.fori_loop(0, parts, finish, 0)


def attend_project(level, counts, mask, order, queries, pieces, wo, x, mod):
    sources, parts, _, heads, rows, _ = pieces.shape
    shards, width = lax.axis_size("tensor"), x.shape[1]
    vmem = pl.BlockSpec(memory_space=pltpu.VMEM)
    hbm = pl.BlockSpec(memory_space=pl.ANY)
    dma = pltpu.SemaphoreType.DMA
    keys = sources * parts * rows
    return pl.pallas_call(
        attend_kernel,
        in_specs=[pl.BlockSpec(memory_space=pltpu.SMEM)] * 4 + [vmem, hbm, hbm, vmem, vmem],
        out_specs=vmem,
        out_shape=jax.ShapeDtypeStruct(x.shape, jnp.bfloat16),
        scratch_shapes=[
            pltpu.VMEM((heads, sources, parts, 2, rows, HEAD_DIM), jnp.bfloat16),
            pltpu.VMEM(wo.shape, jnp.bfloat16),
            pltpu.VMEM((heads, rows, HEAD_DIM), jnp.bfloat16),
        ]
        + [pltpu.VMEM((parts, shards, rows, width), jnp.bfloat16)] * 3
        + [pltpu.VMEM((rows, width), jnp.float32), dma((heads,)), dma]
        + [dma((parts, shards))] * 4,
        compiler_params=pltpu.CompilerParams(vmem_limit_bytes=VMEM_BYTES, collective_id=1, has_side_effects=True),
        cost_estimate=pl.CostEstimate(
            flops=4 * x.shape[0] * keys * heads * HEAD_DIM,
            bytes_accessed=4 * keys * heads * HEAD_DIM,
            transcendentals=x.shape[0] * keys * heads,
        ),
    )(level, counts, mask, order, queries, pieces, wo, x, mod)


def on_device(
    latents,
    w_query,
    w_key,
    w_value,
    w_out,
    query_gain,
    key_gain,
    mod_table,
    levels,
    span_counts,
    block_mask,
    span_order,
):
    modulation = jnp.transpose(mod_table, (1, 0, 2))
    queries, pieces = gather_project(
        levels, latents, modulation, w_query, w_key, w_value, query_gain, key_gain, GATHER_PARTS
    )
    return attend_project(
        levels, span_counts, block_mask, span_order, queries, pieces, w_out, latents, modulation
    )


def solution(mesh):
    return jax.shard_map(
        on_device,
        mesh=mesh,
        in_specs=(
            P("frame", "tensor"),
            P(None, "tensor"),
            P(None, "tensor"),
            P(None, "tensor"),
            P("tensor", None),
            P("tensor", None),
            P("tensor", None),
            P(),
            P("frame"),
            P(),
            P("frame", None),
            P(),
        ),
        out_specs=P("frame", "tensor"),
        check_vma=False,
    )
```
